32 devices in a mesh: gr: 8 (over z, y), gc: 4 (over x, core).
Axes of the slice: x: 2, y: 2, z: 4, core: 2. Of those that a mesh axis runs over, the one named last changes fastest.
Arguments:
- features: bfloat16 [4, 1024, 256], P('gc', 'gr'), may hold values from -6 to 6
- weight: bfloat16 [256, 256], replicated, may hold values from -0.375 to 0.375
- grad_out: bfloat16 [8, 512, 256], P('gr', 'gc'), may hold values from -6 to 6
- block_rows: int32 [8, 4, 6], P('gr', 'gc'), may hold values from 0 to 3, as said below
- block_cols: int32 [8, 4, 6], P('gr', 'gc'), may hold values from 0 to 7
- block_counts: int32 [8, 4], P('gr', 'gc'), may hold values from 1 to 6, as said below
- block_values: bfloat16 [8, 4, 6, 128, 128], P('gr', 'gc'), may hold values from -0.3125 to 0.3125
Outputs:
- activated: bfloat16 [8, 512, 256], P('gr', 'gc')
- grad_weight: float32 [256, 256], replicated
- grad_features: float32 [4, 1024, 256], P('gc', 'gr')
The draws below stay inside these ranges and needn't reach their ends.
Inputs may be any that keep to these rules, and one draw needn't show every extreme that they name: Each tile's block positions (block_rows, block_cols) are distinct over its 6 slots. `block_counts`: some tile has all 6 slots live.
All inputs are finite; a program needn't handle non-finite values.
Results may differ from the reference program's by a relative error of at most 0.03.
Values may be sent and summed in bfloat16 or wider, within the bound.
No kernel may reach another device: no remote copies, remote signals or barrier semaphores. Data moves between devices by JAX's collectives and lax.ppermute only.
A program may use at most 64 MiB of HBM per device.

```python
import jax
import jax.numpy as jnp
from jax import lax

F = 256
BS = 128
R = 128
NODES = 4096
TBR = 4
TBC = 8
MAXB = 6
N_GR = 8
N_GC = 4


def block_positions(key):
    base_key = jax.random.fold_in(key, 7)
    tile_keys = jax.random.split(base_key, N_GR * N_GC)

    def one_tile(tile_key):
        return jax.random.permutation(tile_key, TBR * TBC)[:MAXB].astype(jnp.int32)
    chosen = jax.vmap(one_tile)(tile_keys)
    return chosen.reshape(N_GR, N_GC, MAXB)


def draw_block_rows(key, part):
    return (block_positions(key) // TBC).astype(jnp.int32)


def draw_block_cols(key, part):
    return (block_positions(key) % TBC).astype(jnp.int32)


def draw_block_counts(key, part):
    first_key = jax.random.fold_in(key, 11)
    second_key = jax.random.fold_in(key, 13)
    spread = max(1, 3 * MAXB // 4)
    uneven = jax.random.randint(first_key, (N_GR * N_GC,), 0, spread + 1)
    counts = MAXB // 4 + uneven * uneven // spread
    counts = jnp.clip(counts, 1, MAXB)
    fullest = jax.random.randint(second_key, (), 0, N_GR * N_GC)
    counts = counts.at[fullest].set(MAXB)
    return counts.reshape(N_GR, N_GC).astype(jnp.int32)


def level_of(stream_key, dims, shards, least, top_value):
    def one(position, blocks):
        draws = jax.random.uniform(jax.random.fold_in(jax.random.fold_in(stream_key, 6), position), (blocks,), jnp.float32, least / len(shards), top_value / len(shards))
        return jnp.repeat(jnp.exp(draws), dims[position] // blocks).reshape((-1,) + (1,) * (len(dims) - position - 1))

    factor_of = one(*shards[0])
    for cut in shards[1:]:
        factor_of = factor_of * one(*cut)
    return factor_of


def normal_values(stream_key, dims, scale, bound, shards=(), kind=jnp.bfloat16):
    loudness = level_of(stream_key, dims, shards, -0.22, 0.18) if shards else 1.0
    array = jax.random.normal(stream_key, dims, jnp.float32) * scale * loudness
    return jnp.minimum(jnp.maximum(array, -bound), bound).astype(kind)


def setup_inputs(seed: int = 0) -> dict:
    key_of = jax.random.split(jax.random.key(seed), 8)
    features = normal_values(key_of[0], (N_GC, N_GR * R, F), 1.0, 6.0, ((0, 4), (1, 8)))
    weight = normal_values(key_of[1], (F, F), F ** -0.5, 0.375)
    grad_out = normal_values(key_of[2], (N_GR, N_GC * R, F), 1.0, 6.0, ((0, 8), (1, 4)))
    block_rows = draw_block_rows(jax.random.fold_in(key_of[7], 71), 0)
    block_cols = draw_block_cols(jax.random.fold_in(key_of[7], 71), 0)
    block_counts = draw_block_counts(jax.random.fold_in(key_of[7], 71), 0)
    block_values = normal_values(key_of[6], (N_GR, N_GC, MAXB, BS, BS), (max(1, MAXB * BS * N_GC // (2 * TBR))) ** -0.5, 0.3125, ((0, 8), (1, 4)))
    return {"features": features, "weight": weight, "grad_out": grad_out, "block_rows": block_rows, "block_cols": block_cols, "block_counts": block_counts, "block_values": block_values}


def tile_forward(source, block_values, block_rows, block_cols, live_count):
    live_mask = jnp.arange(MAXB) < live_count
    masked = jnp.where(live_mask[:, None, None], block_values, jnp.zeros_like(block_values))
    picked = source[block_cols]
    products = jnp.einsum('gab,gbf->gaf', masked.astype(jnp.float32), picked.astype(jnp.float32))
    return jnp.zeros((TBR, BS, F), jnp.float32).at[block_rows].add(products)


def tile_backward(source, block_values, block_rows, block_cols, live_count):
    live_mask = jnp.arange(MAXB) < live_count
    masked = jnp.where(live_mask[:, None, None], block_values, jnp.zeros_like(block_values))
    picked = source[block_rows]
    products = jnp.einsum('gba,gbf->gaf', masked.astype(jnp.float32), picked.astype(jnp.float32))
    return jnp.zeros((TBC, BS, F), jnp.float32).at[block_cols].add(products)


def rounded(value):
    return lax.optimization_barrier(value.astype(jnp.bfloat16)).astype(jnp.float32)


def reference(features, weight, grad_out, block_rows, block_cols, block_counts, block_values):
    column_feats = features.reshape(N_GC, TBC, BS, F)

    def forward_tile(running, tile_index):
        row_index = tile_index // N_GC
        col_index = tile_index % N_GC
        partial_rows = tile_forward(column_feats[col_index], block_values[row_index, col_index], block_rows[row_index, col_index], block_cols[row_index, col_index], block_counts[row_index, col_index])
        return running.at[row_index].add(rounded(partial_rows)), None

    aggregated, _ = lax.scan(forward_tile, jnp.zeros((N_GR, TBR, BS, F), jnp.float32), jnp.arange(N_GR * N_GC, dtype=jnp.int32))
    hidden = aggregated.astype(jnp.bfloat16).reshape(NODES, F)
    pre = jnp.dot(hidden, weight, preferred_element_type=jnp.float32)
    activated = jax.nn.silu(pre).astype(jnp.bfloat16)
    sigmoid_pre = jax.nn.sigmoid(pre)
    grad_flat = grad_out.reshape(NODES, F).astype(jnp.float32)
    grad_pre = (grad_flat * sigmoid_pre * (1.0 + pre * (1.0 - sigmoid_pre))).astype(jnp.bfloat16)
    grad_weight = jnp.dot(hidden.T, grad_pre, preferred_element_type=jnp.float32)
    grad_hidden = jnp.dot(grad_pre, weight.T, preferred_element_type=jnp.float32).astype(jnp.bfloat16)
    grad_blocks = grad_hidden.reshape(N_GR, TBR, BS, F)

    def backward_tile(running, tile_index):
        row_index = tile_index // N_GC
        col_index = tile_index % N_GC
        partial_cols = tile_backward(grad_blocks[row_index], block_values[row_index, col_index], block_rows[row_index, col_index], block_cols[row_index, col_index], block_counts[row_index, col_index])
        return running.at[col_index].add(rounded(partial_cols)), None

    grad_total, _ = lax.scan(backward_tile, jnp.zeros((N_GC, TBC, BS, F), jnp.float32), jnp.arange(N_GR * N_GC, dtype=jnp.int32))
    return (activated.reshape(N_GR, N_GC * R, F), grad_weight, grad_total.reshape(N_GC, N_GR * R, F))
```

```python
import functools

import jax
import jax.numpy as jnp
from jax import lax
from jax.experimental import pallas as pl
from jax.experimental.pallas import tpu as pltpu
from jax.sharding import PartitionSpec as P

VMEM = pl.BlockSpec(memory_space=pltpu.VMEM)
SMEM = pl.BlockSpec(memory_space=pltpu.SMEM)
FULL = (((1,), (0,)), ((), ()))
LEFT_T = (((0,), (0,)), ((), ()))
RIGHT_T = (((1,), (1,)), ((), ()))


def f32(value):
    return value.astype(jnp.float32)


def bf16(value):
    return value.astype(jnp.bfloat16)


def swap(value, axis, mask):
    size = lax.axis_size(axis)
    return lax.ppermute(value, axis, [(i, i ^ mask) for i in range(size)])


def bits_of(axis):
    return [1 << b for b in range(lax.axis_size(axis).bit_length() - 1)]


def params(nbytes):
    return pltpu.CompilerParams(vmem_limit_bytes=nbytes)


def per_slot(count, slots, body):
    if slots <= 8:
        for s in range(slots):
            pl.when(s < count)(functools.partial(body, s))
    else:
        lax.fori_loop(0, count, lambda s, _: (body(s), 0)[1], 0)


def forward_kernel(layout, send_masks, keep_masks, info, values, *refs):
    pieces, (send, keep, source, total) = refs[: len(layout)], refs[len(layout):]
    slots, side = values.shape[0], values.shape[1]
    for masks, piece in zip(layout, pieces):
        for n, m in enumerate(masks):
            source[m] = piece[pl.ds(n * side, side), :]
    total[...] = jnp.zeros_like(total)

    def one(s):
        total[info[s]] += lax.dot_general(
            values[s], source[info[slots + s]], FULL, preferred_element_type=jnp.float32
        )

    per_slot(info[2 * slots], slots, one)
    for n, m in enumerate(send_masks):
        send[pl.ds(n * side, side), :] = bf16(total[m])
    for n, m in enumerate(keep_masks):
        keep[pl.ds(n * side, side), :] = bf16(total[m])


def backward_kernel(layout, out_layout, info, values, *refs):
    pieces, rest = refs[: len(layout)], refs[len(layout):]
    outs, (source, total) = rest[: len(out_layout)], rest[len(out_layout):]
    slots, side = values.shape[0], values.shape[1]
    for masks, piece in zip(layout, pieces):
        for n, m in enumerate(masks):
            source[m] = piece[pl.ds(n * side, side), :]
    total[...] = jnp.zeros_like(total)

    def one(s):
        total[info[slots + s]] += lax.dot_general(
            values[s], source[info[s]], LEFT_T, preferred_element_type=jnp.float32
        )

    per_slot(info[2 * slots], slots, one)
    for masks, out in zip(out_layout, outs):
        for n, m in enumerate(masks):
            out[pl.ds(n * side, side), :] = bf16(total[m])


def dense_kernel(mine, near, far, weight, grad_out, activated, hidden, grad_pre, grad_hidden):
    rows = far.shape[0]
    summed = f32(mine[:rows, :]) + f32(near[:rows, :]) + f32(far[...])
    h = bf16(summed)
    w = weight[...]
    pre = lax.dot_general(h, w, FULL, preferred_element_type=jnp.float32)
    s = jax.nn.sigmoid(pre)
    activated[...] = bf16(pre * s)
    g = bf16(f32(grad_out[...]) * s * (1.0 + pre * (1.0 - s)))
    hidden[...] = h
    grad_pre[...] = g
    grad_hidden[...] = bf16(
        lax.dot_general(g, w, RIGHT_T, preferred_element_type=jnp.float32)
    )


def per_device(features, weight, grad_out, block_rows, block_cols, block_counts, block_values):
    side, width = features.shape[1:]
    values = block_values[0, 0]
    slots = values.shape[0]
    gr_size, gc_size = lax.axis_size("gr"), lax.axis_size("gc")
    gr, gc = lax.axis_index("gr"), lax.axis_index("gc")
    outer = [m for m in range(0, gr_size, 2)]
    far_first = sorted(outer[2:]) + [2]
    block = jax.ShapeDtypeStruct((side, width), jnp.bfloat16)

    def stacked(n):
        return jax.ShapeDtypeStruct((n * side, width), jnp.bfloat16)

    limit = 48 * 2**20
    info = jnp.concatenate([block_rows[0, 0] ^ gc, block_cols[0, 0] ^ gr, block_counts[0]])

    with jax.named_scope("gather_features"):
        x = features[0]
        direct = {m: swap(x, "gr", m) for m in far_first}
        near = swap(jnp.concatenate([x, direct[2]], axis=0), "gr", 1)
        sides = {m: swap(direct[m], "gr", 1) for m in far_first[:-1]}
    layout = [(0,), (2,), (1, 3)]
    pieces = [x, direct[2], near]
    for m in far_first[:-1]:
        layout += [(m,), (m + 1,)]
        pieces += [direct[m], sides[m]]

    with jax.named_scope("forward_blocks"):
        send_masks = [m for m in range(gc_size) if m & 1]
        keep_masks = [m for m in range(gc_size) if not m & 1]
        send, keep = pl.pallas_call(
            functools.partial(forward_kernel, layout, send_masks, keep_masks),
            out_shape=[stacked(len(send_masks)), stacked(len(keep_masks))],
            in_specs=[SMEM] + [VMEM] * (1 + len(pieces)),
            out_specs=[VMEM, VMEM],
            scratch_shapes=[
                pltpu.VMEM((gr_size, side, width), jnp.bfloat16),
                pltpu.VMEM((gc_size, side, width), jnp.float32),
            ],
            compiler_params=params(limit),
        )(info, values, *pieces)

    with jax.named_scope("sum_rows"):
        got = swap(send, "gc", 1)
        held = len(keep_masks)
        for bit in reversed(bits_of("gc")[1:]):
            half = held // 2 * side
            outgoing = bf16(f32(keep[half:]) + f32(got[half:]))
            if held > 2:
                keep = bf16(f32(keep[:half]) + f32(got[:half]))
                got = swap(outgoing, "gc", bit)
            else:
                last = swap(outgoing, "gc", bit)
            held //= 2

    with jax.named_scope("dense"):
        activated, hidden, grad_pre, grad_hidden = pl.pallas_call(
            dense_kernel,
            out_shape=[block] * 4,
            in_specs=[VMEM] * 5,
            out_specs=[VMEM] * 4,
            compiler_params=params(limit),
        )(keep, got, last, weight, grad_out[0])

    with jax.named_scope("gather_grad_hidden"):
        held = {0: grad_hidden}
        for bit in reversed(bits_of("gc")):
            held.update({m | bit: swap(v, "gc", bit) for m, v in list(held.items())})

    with jax.named_scope("backward_blocks"):
        far = far_first[:-1]
        out_layout = [tuple(m + 1 for m in far), (3, 1), tuple(far), (2, 0)]
        far_send, near_send, far_keep, near_keep = pl.pallas_call(
            functools.partial(backward_kernel, [(m,) for m in held], out_layout),
            out_shape=[stacked(len(masks)) for masks in out_layout],
            in_specs=[SMEM] + [VMEM] * (1 + len(held)),
            out_specs=[VMEM] * 4,
            scratch_shapes=[
                pltpu.VMEM((gc_size, side, width), jnp.bfloat16),
                pltpu.VMEM((gr_size, side, width), jnp.float32),
            ],
            compiler_params=params(limit),
        )(info, values, *held.values())

    with jax.named_scope("sum_columns"):
        far_got = swap(far_send, "gr", 1)
        near_got = swap(near_send, "gr", 1)
        terms = []
        for n, m in enumerate(far):
            rows = slice(n * side, (n + 1) * side)
            terms.append(swap(bf16(f32(far_keep[rows]) + f32(far_got[rows])), "gr", m))
        terms.append(swap(bf16(f32(near_keep[:side]) + f32(near_got[:side])), "gr", 2))
        grad_features = f32(near_keep[side:]) + f32(near_got[side:])
        for term in terms:
            grad_features = grad_features + f32(term)

    with jax.named_scope("sum_weight"):
        local = bf16(lax.dot_general(hidden, grad_pre, LEFT_T, preferred_element_type=jnp.float32))
        half = width // 2
        upper = (gc & 1) == 0
        top, bottom = local[:half], local[half:]
        running = f32(jnp.where(upper, top, bottom)) + f32(
            swap(jnp.where(upper, bottom, top), "gc", 1)
        )
        for axis, bits in (("gc", bits_of("gc")[1:]), ("gr", bits_of("gr"))):
            for bit in bits:
                mine = bf16(running)
                running = f32(mine) + f32(swap(mine, axis, bit))
        other = swap(running, "gc", 1)
        grad_weight = jnp.where(
            upper, jnp.concatenate([running, other]), jnp.concatenate([other, running])
        )
    return activated[None], grad_weight, grad_features[None]


def solution(mesh):
    placed = (
        P("gc", "gr", None),
        P(),
        P("gr", "gc", None),
        P("gr", "gc", None),
        P("gr", "gc", None),
        P("gr", "gc"),
        P("gr", "gc", None, None, None),
    )
    return jax.shard_map(
        per_device,
        mesh=mesh,
        in_specs=placed,
        out_specs=(P("gr", "gc", None), P(), P("gc", "gr", None)),
        check_vma=False,
    )
```

```python
import functools

import jax
import jax.numpy as jnp
from jax import lax
from jax.experimental import pallas as pl
from jax.experimental.pallas import tpu as pltpu
from jax.sharding import PartitionSpec as P

VMEM = pl.BlockSpec(memory_space=pltpu.VMEM)
SMEM = pl.BlockSpec(memory_space=pltpu.SMEM)
FULL = (((1,), (0,)), ((), ()))
LEFT_T = (((0,), (0,)), ((), ()))
RIGHT_T = (((1,), (1,)), ((), ()))


def f32(value):
    return value.astype(jnp.float32)


def bf16(value):
    return value.astype(jnp.bfloat16)


def swap(value, axis, mask):
    size = lax.axis_size(axis)
    return lax.ppermute(value, axis, [(i, i ^ mask) for i in range(size)])


def bits_of(axis):
    return [1 << b for b in range(lax.axis_size(axis).bit_length() - 1)]


def after(value, *deps):
    return lax.optimization_barrier((value, *deps))[0]


class Line:
    def __init__(self):
        self.last = None

    def __call__(self, value):
        self.last = value if self.last is None else after(value, self.last)
        return self.last


def params(nbytes):
    return pltpu.CompilerParams(vmem_limit_bytes=nbytes)


def slot_products(transposed, info, values, source, total):
    slots = values.shape[0]
    count = info[2, 0]
    dims = LEFT_T if transposed else FULL

    def place(s):
        row, col = info[0, s], info[1, s]
        return (row, col) if transposed else (col, row)

    def product(s):
        return lax.dot_general(
            values[s], source[place(s)[0]], dims, preferred_element_type=jnp.float32
        )

    total[...] = jnp.zeros_like(total)
    if slots <= 8:
        products = [product(s) for s in range(slots)]
        for s in range(slots):
            total[place(s)[1]] += jnp.where(s < count, products[s], 0.0)
    else:

        def one(s, _):
            total[place(s)[1]] += product(s)
            return 0

        lax.fori_loop(0, count, one, 0)


def info_kernel(rows, cols, counts, info):
    slots = rows.shape[1]
    info[...] = jnp.zeros_like(info)
    info[0:1, pl.ds(0, slots)] = rows[...] ^ lax.axis_index("gc")
    info[1:2, pl.ds(0, slots)] = cols[...] ^ lax.axis_index("gr")
    info[2:3, pl.ds(0, 1)] = counts[...]


def forward_kernel(layout, send_masks, keep_masks, info, values, *refs):
    pieces, (send, keep, source, total) = refs[: len(layout)], refs[len(layout):]
    side = values.shape[1]
    for masks, piece in zip(layout, pieces):
        for n, m in enumerate(masks):
            source[m] = piece[pl.ds(n * side, side), :]
    slot_products(False, info, values, source, total)
    for n, m in enumerate(send_masks):
        send[pl.ds(n * side, side), :] = bf16(total[m])
    for n, m in enumerate(keep_masks):
        keep[pl.ds(n * side, side), :] = bf16(total[m])


def backward_kernel(layout, out_layout, info, values, *refs):
    pieces, rest = refs[: len(layout)], refs[len(layout):]
    outs, (source, total) = rest[: len(out_layout)], rest[len(out_layout):]
    side = values.shape[1]
    for masks, piece in zip(layout, pieces):
        for n, m in enumerate(masks):
            source[m] = piece[pl.ds(n * side, side), :]
    slot_products(True, info, values, source, total)
    for masks, out in zip(out_layout, outs):
        for n, m in enumerate(masks):
            out[pl.ds(n * side, side), :] = bf16(total[m])


def dense_kernel(bit, mine, got, weight, *refs):
    *grads, activated, message, kept, total = refs
    side, half = activated.shape[0], kept.shape[0]
    blocks = mine.shape[0] // side
    w = weight[...]
    summed = [
        f32(mine[pl.ds(e * side, side), :]) + f32(got[pl.ds((e ^ bit) * side, side), :])
        for e in range(blocks)
    ]
    hidden = bf16(jnp.concatenate(summed))
    pre = lax.dot_general(hidden, w, FULL, preferred_element_type=jnp.float32)
    s = 1.0 / (1.0 + jnp.exp(-pre))
    activated[...] = bf16(pre[:side] * s[:side])
    grad_out = jnp.concatenate([f32(g[...]) for g in grads])
    grad_pre = bf16(grad_out * s * (1.0 + pre * (1.0 - s)))
    message[pl.ds(0, blocks * side), :] = bf16(
        lax.dot_general(grad_pre, w, RIGHT_T, preferred_element_type=jnp.float32)
    )
    total[...] = lax.dot_general(hidden, grad_pre, LEFT_T, preferred_element_type=jnp.float32)
    place = lax.axis_index("gc") & 1
    kept[...] = total[pl.ds(pl.multiple_of(place * half, half), half), :]
    message[pl.ds(blocks * side, half), :] = bf16(
        total[pl.ds(pl.multiple_of((1 - place) * half, half), half), :]
    )


def finish_kernel(mine, other, *refs):
    (kept, part, *terms), (grad_features, grad_weight) = refs[:-2], refs[-2:]
    side = grad_features.shape[0]
    parts = [f32(v[pl.ds(side, side), :]) for v in (kept, part)] + [f32(t[...]) for t in terms]
    grad_features[...] = functools.reduce(lambda a, b: a + b, parts)
    half = mine.shape[0]
    place = lax.axis_index("gc") & 1
    grad_weight[pl.ds(pl.multiple_of(place * half, half), half), :] = f32(mine[...])
    grad_weight[pl.ds(pl.multiple_of((1 - place) * half, half), half), :] = f32(other[...])


def per_device(features, weight, grad_out, block_rows, block_cols, block_counts, block_values):
    side, width = features.shape[1:]
    gr_size, gc_size = lax.axis_size("gr"), lax.axis_size("gc")
    outer = [m for m in range(0, gr_size, 2)]
    far_first = sorted(outer[2:]) + [2]
    block = jax.ShapeDtypeStruct((side, width), jnp.bfloat16)

    def stacked(n):
        return jax.ShapeDtypeStruct((n * side, width), jnp.bfloat16)

    limit = 48 * 2**20
    with jax.named_scope("gather_features"):
        x = features[0]
        moved = {m: swap(x, "gr", m) for m in far_first + [1]}
        arrival = Line()
        held = {}
        for m in far_first[:1] + [2] + far_first[1:-1] + [1]:
            held[m] = arrival(moved[m])
            if m > 1:
                moved[m + 1] = swap(held[m], "gr", 1)
        values = block_values[0, 0]
        info = pl.pallas_call(
            info_kernel,
            out_shape=jax.ShapeDtypeStruct((8, 128 * pl.cdiv(values.shape[0], 128)), jnp.int32),
            in_specs=[VMEM] * 3,
            out_specs=VMEM,
            compiler_params=params(limit),
            cost_estimate=pl.CostEstimate(flops=5 * 10**9, bytes_accessed=0, transcendentals=0),
        )(after(block_rows[0], held[2]), block_cols[0], block_counts)
        grads = {0: after(grad_out[0], held[1])}
        for bit in bits_of("gc")[1:]:
            grads.update({m | bit: swap(v, "gc", bit) for m, v in list(grads.items())})
        grads = {m: arrival(v) for m, v in grads.items()}
        for m in (far_first[:1] + [2] + far_first[1:-1])[::-1]:
            held[m + 1] = arrival(moved[m + 1])
        held[0] = x
    layout = [(m,) for m in held]
    pieces = list(held.values())
    pieces[0] = after(pieces[0], *grads.values())

    with jax.named_scope("forward_blocks"):
        send_masks = [m for m in range(gc_size) if m & 1]
        keep_masks = [m for m in range(gc_size) if not m & 1]
        send, keep = pl.pallas_call(
            functools.partial(forward_kernel, layout, send_masks, keep_masks),
            out_shape=[stacked(len(send_masks)), stacked(len(keep_masks))],
            in_specs=[SMEM] + [VMEM] * (1 + len(pieces)),
            out_specs=[VMEM, VMEM],
            scratch_shapes=[
                pltpu.VMEM((gr_size, side, width), jnp.bfloat16),
                pltpu.VMEM((gc_size, side, width), jnp.float32),
            ],
            compiler_params=params(limit),
        )(info, values, *pieces)

    with jax.named_scope("sum_rows"):
        near = swap(send, "gc", 1)
        mine = bf16(f32(keep) + f32(near))
        *bits, last = bits_of("gc")[1:]
        for bit in bits:
            order = jnp.arange(len(keep_masks)) ^ (bit >> 1)
            got = swap(mine, "gc", bit).reshape(-1, side, width)[order].reshape(mine.shape)
            mine = bf16(f32(mine) + f32(got))
        got = swap(mine, "gc", last)

    half = width // 2
    with jax.named_scope("dense"):
        activated, message, kept = pl.pallas_call(
            functools.partial(dense_kernel, last >> 1),
            out_shape=[
                block,
                jax.ShapeDtypeStruct((mine.shape[0] + half, width), jnp.bfloat16),
                jax.ShapeDtypeStruct((half, width), jnp.float32),
            ],
            in_specs=[VMEM] * (3 + len(grads)),
            out_specs=[VMEM] * 3,
            scratch_shapes=[pltpu.VMEM((width, width), jnp.float32)],
            compiler_params=params(limit),
        )(mine, got, weight, *[grads[m] for m in keep_masks])

    with jax.named_scope("swap_cores"):
        answer = swap(message, "gc", 1)
        running = kept + f32(answer[mine.shape[0]:])
    stages = [("gr", bit) for bit in bits_of("gr")[:0:-1] + [1]]
    sent, got, order = [], [], Line()

    def launch(running):
        with jax.named_scope("sum_weight"):
            sent.append(bf16(running))
            got.append(swap(sent[-1], *stages[len(sent) - 1]))

    def advance():
        if len(sent) > len(stages):
            return
        with jax.named_scope("sum_weight"):
            running = f32(sent[-1]) + f32(order(got[-1]))
            if len(sent) < len(stages):
                launch(running)
            else:
                sent.append(bf16(running))
                got.append(swap(sent[-1], "gc", 1))

    launch(running)

    with jax.named_scope("backward_blocks"):
        kept_masks = [(m,) for m in far_first[:-1]] + [(2, 0)]
        out_layout = [tuple(m + 1 for m in masks) for masks in kept_masks] + kept_masks
        outs = pl.pallas_call(
            functools.partial(backward_kernel, [keep_masks, send_masks], out_layout),
            out_shape=[stacked(len(masks)) for masks in out_layout],
            in_specs=[SMEM] + [VMEM] * 3,
            out_specs=[VMEM] * len(out_layout),
            scratch_shapes=[
                pltpu.VMEM((gc_size, side, width), jnp.bfloat16),
                pltpu.VMEM((gr_size, side, width), jnp.float32),
            ],
            compiler_params=params(limit),
        )(info, values, message, answer)
        sends, keeps = outs[: len(kept_masks)], outs[len(kept_masks):]

    with jax.named_scope("sum_columns"):
        arrived = [swap(v, "gr", 1) for v in sends]
        order(keeps[0])
        advance()
        terms = []
        for masks, kept, part in zip(kept_masks[:-1], keeps, arrived):
            total = bf16(f32(kept) + f32(order(part)))
            terms.append(swap(total, "gr", masks[0]))
        advance()
        own = (keeps[-1], order(arrived[-1]))
        total = bf16(f32(own[0][:side]) + f32(own[1][:side]))
        terms.append(swap(total, "gr", 2))
    while len(sent) <= len(stages):
        advance()
    terms = [order(term) for term in terms]
    running, other = sent[-1], order(got[-1])

    grad_features, grad_weight = pl.pallas_call(
        finish_kernel,
        out_shape=[
            jax.ShapeDtypeStruct((side, width), jnp.float32),
            jax.ShapeDtypeStruct((width, width), jnp.float32),
        ],
        in_specs=[VMEM] * (4 + len(terms)),
        out_specs=[VMEM] * 2,
        compiler_params=params(limit),
    )(running, other, *own, *terms)
    return activated[None], grad_weight, grad_features[None]


def solution(mesh):
    placed = (
        P("gc", "gr", None),
        P(),
        P("gr", "gc", None),
        P("gr", "gc", None),
        P("gr", "gc", None),
        P("gr", "gc"),
        P("gr", "gc", None, None, None),
    )
    return jax.shard_map(
        per_device,
        mesh=mesh,
        in_specs=placed,
        out_specs=(P("gr", "gc", None), P(), P("gc", "gr", None)),
        check_vma=False,
    )
```

```python
import functools

import jax
import jax.numpy as jnp
from jax import lax
from jax.experimental import pallas as pl
from jax.experimental.pallas import tpu as pltpu
from jax.sharding import PartitionSpec as P

VMEM = pl.BlockSpec(memory_space=pltpu.VMEM)
SMEM = pl.BlockSpec(memory_space=pltpu.SMEM)
FULL = (((1,), (0,)), ((), ()))
LEFT_T = (((0,), (0,)), ((), ()))
RIGHT_T = (((1,), (1,)), ((), ()))


def f32(value):
    return value.astype(jnp.float32)


def bf16(value):
    return value.astype(jnp.bfloat16)


def swap(value, axis, mask):
    size = lax.axis_size(axis)
    return lax.ppermute(value, axis, [(i, i ^ mask) for i in range(size)])


def bits_of(axis):
    return [1 << b for b in range(lax.axis_size(axis).bit_length() - 1)]


def after(value, *deps):
    return lax.optimization_barrier((value, *deps))[0]


class Line:
    def __init__(self):
        self.last = None

    def __call__(self, value):
        self.last = value if self.last is None else after(value, self.last)
        return self.last


def params(nbytes):
    return pltpu.CompilerParams(vmem_limit_bytes=nbytes)


def slot_products(transposed, info, values, source, total):
    slots = values.shape[0]
    count = info[2, 0]
    dims = LEFT_T if transposed else FULL

    def place(s):
        row, col = info[0, s], info[1, s]
        return (row, col) if transposed else (col, row)

    def product(s):
        return lax.dot_general(
            values[s], source[place(s)[0]], dims, preferred_element_type=jnp.float32
        )

    total[...] = jnp.zeros_like(total)
    if slots <= 8:
        products = [product(s) for s in range(slots)]
        for s in range(slots):
            total[place(s)[1]] += jnp.where(s < count, products[s], 0.0)
    else:

        def one(s, _):
            total[place(s)[1]] += product(s)
            return 0

        lax.fori_loop(0, count, one, 0)


def join_kernel(*refs):
    *parts, out = refs
    rows = parts[0].shape[0]
    for n, part in enumerate(parts):
        out[pl.ds(n * rows, rows), :] = part[...]


def join(*parts):
    shape = (len(parts) * parts[0].shape[0], parts[0].shape[1])
    return pl.pallas_call(
        join_kernel,
        out_shape=jax.ShapeDtypeStruct(shape, parts[0].dtype),
        in_specs=[VMEM] * len(parts),
        out_specs=VMEM,
        compiler_params=params(16 * 2**20),
    )(*parts)


def info_kernel(rows, cols, counts, info):
    slots = rows.shape[1]
    info[...] = jnp.zeros_like(info)
    info[0:1, pl.ds(0, slots)] = rows[...] ^ lax.axis_index("gc")
    info[1:2, pl.ds(0, slots)] = cols[...] ^ lax.axis_index("gr")
    info[2:3, pl.ds(0, 1)] = counts[...]


def forward_kernel(layout, send_masks, keep_masks, info, values, *refs):
    pieces, (send, keep, source, total) = refs[: len(layout)], refs[len(layout):]
    side = values.shape[1]
    for masks, piece in zip(layout, pieces):
        for n, m in enumerate(masks):
            source[m] = piece[pl.ds(n * side, side), :]
    slot_products(False, info, values, source, total)
    for n, m in enumerate(send_masks):
        send[pl.ds(n * side, side), :] = bf16(total[m])
    for n, m in enumerate(keep_masks):
        keep[pl.ds(n * side, side), :] = bf16(total[m])


def backward_kernel(layout, out_layout, info, values, *refs):
    pieces, rest = refs[: len(layout)], refs[len(layout):]
    outs, (source, total) = rest[: len(out_layout)], rest[len(out_layout):]
    side = values.shape[1]
    for masks, piece in zip(layout, pieces):
        for n, m in enumerate(masks):
            source[m] = piece[pl.ds(n * side, side), :]
    slot_products(True, info, values, source, total)
    for masks, out in zip(out_layout, outs):
        for n, m in enumerate(masks):
            out[pl.ds(n * side, side), :] = bf16(total[m])


def dense_kernel(bit, mine, got, weight, *refs):
    *grads, activated, message, kept, total = refs
    side, half = activated.shape[0], kept.shape[0]
    blocks = mine.shape[0] // side
    w = weight[...]
    summed = [
        f32(mine[pl.ds(e * side, side), :]) + f32(got[pl.ds((e ^ bit) * side, side), :])
        for e in range(blocks)
    ]
    hidden = bf16(jnp.concatenate(summed))
    pre = lax.dot_general(hidden, w, FULL, preferred_element_type=jnp.float32)
    s = 1.0 / (1.0 + jnp.exp(-pre))
    activated[...] = bf16(pre[:side] * s[:side])
    grad_out = jnp.concatenate([f32(g[...]) for g in grads])
    grad_pre = bf16(grad_out * s * (1.0 + pre * (1.0 - s)))
    message[pl.ds(0, blocks * side), :] = bf16(
        lax.dot_general(grad_pre, w, RIGHT_T, preferred_element_type=jnp.float32)
    )
    total[...] = lax.dot_general(hidden, grad_pre, LEFT_T, preferred_element_type=jnp.float32)
    place = lax.axis_index("gc") & 1
    kept[...] = total[pl.ds(pl.multiple_of(place * half, half), half), :]
    message[pl.ds(blocks * side, half), :] = bf16(
        total[pl.ds(pl.multiple_of((1 - place) * half, half), half), :]
    )


def finish_kernel(mine, other, *refs):
    (kept, part, *terms), (grad_features, grad_weight) = refs[:-2], refs[-2:]
    side = grad_features.shape[0]
    parts = [f32(v[pl.ds(side, side), :]) for v in (kept, part)] + [f32(t[...]) for t in terms]
    grad_features[...] = functools.reduce(lambda a, b: a + b, parts)
    half = mine.shape[0]
    place = lax.axis_index("gc") & 1
    grad_weight[pl.ds(pl.multiple_of(place * half, half), half), :] = f32(mine[...])
    grad_weight[pl.ds(pl.multiple_of((1 - place) * half, half), half), :] = f32(other[...])


def per_device(features, weight, grad_out, block_rows, block_cols, block_counts, block_values):
    side, width = features.shape[1:]
    gr_size, gc_size = lax.axis_size("gr"), lax.axis_size("gc")
    outer = [m for m in range(0, gr_size, 2)]
    far_first = sorted(outer[2:]) + [2]
    block = jax.ShapeDtypeStruct((side, width), jnp.bfloat16)

    def stacked(n):
        return jax.ShapeDtypeStruct((n * side, width), jnp.bfloat16)

    limit = 48 * 2**20
    with jax.named_scope("gather_features"):
        x = features[0]
        first, *others = far_first[:-1]
        held = {m: swap(x, "gr", m) for m in [1, first, 2, *others]}
        held[0] = x
        grads = {0: after(grad_out[0], held[2])}
        for bit in bits_of("gc")[1:]:
            grads.update({m | bit: swap(v, "gc", bit) for m, v in list(grads.items())})
        held.update({m + 1: swap(held[m], "gr", 1) for m in [first, 2, *others]})
        values = block_values[0, 0]
        info = pl.pallas_call(
            info_kernel,
            out_shape=jax.ShapeDtypeStruct((8, 128 * pl.cdiv(values.shape[0], 128)), jnp.int32),
            in_specs=[VMEM] * 3,
            out_specs=VMEM,
            compiler_params=params(limit),
            cost_estimate=pl.CostEstimate(flops=5 * 10**9, bytes_accessed=0, transcendentals=0),
        )(*[after(v, held[2]) for v in (block_rows[0], block_cols[0], block_counts)])
    layout = [(m,) for m in held]
    held[0] = after(x, *grads.values())
    pieces = list(held.values())

    with jax.named_scope("forward_blocks"):
        send_masks = [m for m in range(gc_size) if m & 1]
        keep_masks = [m for m in range(gc_size) if not m & 1]
        send, keep = pl.pallas_call(
            functools.partial(forward_kernel, layout, send_masks, keep_masks),
            out_shape=[stacked(len(send_masks)), stacked(len(keep_masks))],
            in_specs=[SMEM] + [VMEM] * (1 + len(pieces)),
            out_specs=[VMEM, VMEM],
            scratch_shapes=[
                pltpu.VMEM((gr_size, side, width), jnp.bfloat16),
                pltpu.VMEM((gc_size, side, width), jnp.float32),
            ],
            compiler_params=params(limit),
        )(info, values, *pieces)

    with jax.named_scope("sum_rows"):
        near = swap(send, "gc", 1)
        mine = bf16(f32(keep) + f32(near))
        *bits, last = bits_of("gc")[1:]
        for bit in bits:
            order = jnp.arange(len(keep_masks)) ^ (bit >> 1)
            got = swap(mine, "gc", bit).reshape(-1, side, width)[order].reshape(mine.shape)
            mine = bf16(f32(mine) + f32(got))
        got = swap(mine, "gc", last)

    half = width // 2
    with jax.named_scope("dense"):
        activated, message, kept = pl.pallas_call(
            functools.partial(dense_kernel, last >> 1),
            out_shape=[
                block,
                jax.ShapeDtypeStruct((mine.shape[0] + half, width), jnp.bfloat16),
                jax.ShapeDtypeStruct((half, width), jnp.float32),
            ],
            in_specs=[VMEM] * (3 + len(grads)),
            out_specs=[VMEM] * 3,
            scratch_shapes=[pltpu.VMEM((width, width), jnp.float32)],
            compiler_params=params(limit),
        )(mine, got, weight, *[grads[m] for m in keep_masks])

    with jax.named_scope("swap_cores"):
        answer = swap(message, "gc", 1)
        running = kept + f32(answer[mine.shape[0]:])
    stages = [("gr", bit) for bit in bits_of("gr")[:0:-1] + [1]]
    sent, got, order = [], [], Line()

    def launch(running):
        with jax.named_scope("sum_weight"):
            sent.append(bf16(running))
            got.append(swap(sent[-1], *stages[len(sent) - 1]))

    def advance():
        if len(sent) > len(stages):
            return
        with jax.named_scope("sum_weight"):
            running = f32(sent[-1]) + f32(order(got[-1]))
            if len(sent) < len(stages):
                launch(running)
            else:
                sent.append(bf16(running))
                got.append(swap(sent[-1], "gc", 1))

    launch(running)

    with jax.named_scope("backward_blocks"):
        kept_masks = [(m,) for m in far_first[:-1]] + [(2, 0)]
        out_layout = [tuple(m + 1 for m in masks) for masks in kept_masks] + kept_masks
        outs = pl.pallas_call(
            functools.partial(backward_kernel, [keep_masks, send_masks], out_layout),
            out_shape=[stacked(len(masks)) for masks in out_layout],
            in_specs=[SMEM] + [VMEM] * 3,
            out_specs=[VMEM] * len(out_layout),
            scratch_shapes=[
                pltpu.VMEM((gc_size, side, width), jnp.bfloat16),
                pltpu.VMEM((gr_size, side, width), jnp.float32),
            ],
            compiler_params=params(limit),
        )(info, values, message, answer)
        sends, keeps = outs[: len(kept_masks)], outs[len(kept_masks):]

    with jax.named_scope("sum_columns"):
        arrived = [swap(v, "gr", 1) for v in sends]
        order(keeps[0])
        advance()
        terms = []
        for masks, kept, part in zip(kept_masks[:-1], keeps, arrived):
            total = bf16(f32(kept) + f32(order(part)))
            terms.append(swap(total, "gr", masks[0]))
        advance()
        own = (keeps[-1], order(arrived[-1]))
        total = bf16(f32(own[0][:side]) + f32(own[1][:side]))
        terms.append(swap(total, "gr", 2))
    while len(sent) <= len(stages):
        advance()
    terms = [order(term) for term in terms]
    running, other = sent[-1], order(got[-1])

    grad_features, grad_weight = pl.pallas_call(
        finish_kernel,
        out_shape=[
            jax.ShapeDtypeStruct((side, width), jnp.float32),
            jax.ShapeDtypeStruct((width, width), jnp.float32),
        ],
        in_specs=[VMEM] * (4 + len(terms)),
        out_specs=[VMEM] * 2,
        compiler_params=params(limit),
    )(running, other, *own, *terms)
    return activated[None], grad_weight, grad_features[None]


def solution(mesh):
    placed = (
        P("gc", "gr", None),
        P(),
        P("gr", "gc", None),
        P("gr", "gc", None),
        P("gr", "gc", None),
        P("gr", "gc"),
        P("gr", "gc", None, None, None),
    )
    return jax.shard_map(
        per_device,
        mesh=mesh,
        in_specs=placed,
        out_specs=(P("gr", "gc", None), P(), P("gc", "gr", None)),
        check_vma=False,
    )
```

```python
import functools

import jax
import jax.numpy as jnp
from jax import lax
from jax.experimental import pallas as pl
from jax.experimental.pallas import tpu as pltpu
from jax.sharding import PartitionSpec as P

VMEM = pl.BlockSpec(memory_space=pltpu.VMEM)
SMEM = pl.BlockSpec(memory_space=pltpu.SMEM)
FULL = (((1,), (0,)), ((), ()))
LEFT_T = (((0,), (0,)), ((), ()))
RIGHT_T = (((1,), (1,)), ((), ()))


def f32(value):
    return value.astype(jnp.float32)


def bf16(value):
    return value.astype(jnp.bfloat16)


def swap(value, axis, mask):
    size = lax.axis_size(axis)
    return lax.ppermute(value, axis, [(i, i ^ mask) for i in range(size)])


def swap_crossed(value, mask):
    rows, cols = lax.axis_size("gr"), lax.axis_size("gc")
    pairs = [
        (r * cols + c, (r ^ mask) * cols + (c ^ 1)) for r in range(rows) for c in range(cols)
    ]
    return lax.ppermute(value, ("gr", "gc"), pairs)


def weight_half():
    half, rows = lax.axis_index("gc"), lax.axis_index("gr")
    for b in range(lax.axis_size("gr").bit_length() - 1):
        half = half ^ (rows >> b)
    return half & 1


def bits_of(axis):
    return [1 << b for b in range(lax.axis_size(axis).bit_length() - 1)]


def after(value, *deps):
    return lax.optimization_barrier((value, *deps))[0]


class Line:
    def __init__(self):
        self.last = None

    def __call__(self, value):
        self.last = value if self.last is None else after(value, self.last)
        return self.last


def params(nbytes):
    return pltpu.CompilerParams(vmem_limit_bytes=nbytes)


def slot_products(transposed, info, values, source, total):
    slots = values.shape[0]
    count = info[2, 0]
    dims = LEFT_T if transposed else FULL

    def place(s):
        row, col = info[0, s], info[1, s]
        return (row, col) if transposed else (col, row)

    def product(s):
        return lax.dot_general(
            values[s], source[place(s)[0]], dims, preferred_element_type=jnp.float32
        )

    total[...] = jnp.zeros_like(total)
    if slots <= 8:
        products = [product(s) for s in range(slots)]
        for s in range(slots):
            total[place(s)[1]] += jnp.where(s < count, products[s], 0.0)
    else:

        def one(s, _):
            total[place(s)[1]] += product(s)
            return 0

        lax.fori_loop(0, count, one, 0)


def join_kernel(*refs):
    *parts, out = refs
    rows = parts[0].shape[0]
    for n, part in enumerate(parts):
        out[pl.ds(n * rows, rows), :] = part[...]


def join(*parts):
    shape = (len(parts) * parts[0].shape[0], parts[0].shape[1])
    return pl.pallas_call(
        join_kernel,
        out_shape=jax.ShapeDtypeStruct(shape, parts[0].dtype),
        in_specs=[VMEM] * len(parts),
        out_specs=VMEM,
        compiler_params=params(16 * 2**20),
    )(*parts)


def info_kernel(rows, cols, counts, info):
    slots = rows.shape[1]
    info[...] = jnp.zeros_like(info)
    info[0:1, pl.ds(0, slots)] = rows[...] ^ lax.axis_index("gc")
    info[1:2, pl.ds(0, slots)] = cols[...] ^ lax.axis_index("gr")
    info[2:3, pl.ds(0, 1)] = counts[...]


def forward_kernel(layout, send_masks, keep_masks, info, values, *refs):
    pieces, (send, keep, source, total) = refs[: len(layout)], refs[len(layout):]
    side = values.shape[1]
    for masks, piece in zip(layout, pieces):
        for n, m in enumerate(masks):
            source[m] = piece[pl.ds(n * side, side), :]
    slot_products(False, info, values, source, total)
    for n, m in enumerate(send_masks):
        send[pl.ds(n * side, side), :] = bf16(total[m])
    for n, m in enumerate(keep_masks):
        keep[pl.ds(n * side, side), :] = bf16(total[m])


def backward_kernel(layout, out_layout, info, values, *refs):
    pieces, rest = refs[: len(layout)], refs[len(layout):]
    outs, (source, total) = rest[: len(out_layout)], rest[len(out_layout):]
    side = values.shape[1]
    for masks, piece in zip(layout, pieces):
        for n, m in enumerate(masks):
            source[m] = piece[pl.ds(n * side, side), :]
    slot_products(True, info, values, source, total)
    for masks, out in zip(out_layout, outs):
        for n, m in enumerate(masks):
            out[pl.ds(n * side, side), :] = bf16(total[m])


def dense_kernel(bit, mine, got, weight, *refs):
    *grads, activated, message, kept, total = refs
    side, half = activated.shape[0], kept.shape[0]
    blocks = mine.shape[0] // side
    w = weight[...]
    summed = [
        f32(mine[pl.ds(e * side, side), :]) + f32(got[pl.ds((e ^ bit) * side, side), :])
        for e in range(blocks)
    ]
    hidden = bf16(jnp.concatenate(summed))
    pre = lax.dot_general(hidden, w, FULL, preferred_element_type=jnp.float32)
    s = 1.0 / (1.0 + jnp.exp(-pre))
    activated[...] = bf16(pre[:side] * s[:side])
    grad_out = jnp.concatenate([f32(g[...]) for g in grads])
    grad_pre = bf16(grad_out * s * (1.0 + pre * (1.0 - s)))
    message[pl.ds(0, blocks * side), :] = bf16(
        lax.dot_general(grad_pre, w, RIGHT_T, preferred_element_type=jnp.float32)
    )
    total[...] = lax.dot_general(hidden, grad_pre, LEFT_T, preferred_element_type=jnp.float32)
    place = weight_half()
    kept[...] = total[pl.ds(pl.multiple_of(place * half, half), half), :]
    message[pl.ds(blocks * side, half), :] = bf16(
        total[pl.ds(pl.multiple_of((1 - place) * half, half), half), :]
    )


def finish_kernel(mine, other, *refs):
    (kept, part, *terms), (grad_features, grad_weight) = refs[:-2], refs[-2:]
    side = grad_features.shape[0]
    parts = [f32(v[pl.ds(side, side), :]) for v in (kept, part)] + [f32(t[...]) for t in terms]
    grad_features[...] = functools.reduce(lambda a, b: a + b, parts)
    half = mine.shape[0]
    place = weight_half()
    grad_weight[pl.ds(pl.multiple_of(place * half, half), half), :] = f32(mine[...])
    grad_weight[pl.ds(pl.multiple_of((1 - place) * half, half), half), :] = f32(other[...])


def per_device(features, weight, grad_out, block_rows, block_cols, block_counts, block_values):
    side, width = features.shape[1:]
    gr_size, gc_size = lax.axis_size("gr"), lax.axis_size("gc")
    outer = [m for m in range(0, gr_size, 2)]
    far_first = sorted(outer[2:]) + [2]
    block = jax.ShapeDtypeStruct((side, width), jnp.bfloat16)

    def stacked(n):
        return jax.ShapeDtypeStruct((n * side, width), jnp.bfloat16)

    limit = 48 * 2**20
    with jax.named_scope("gather_features"):
        x = features[0]
        first, *others = far_first[:-1]
        held = {m: swap(x, "gr", m) for m in [1, first, 2, *others]}
        held[0] = x
        grads = {0: after(grad_out[0], held[2])}
        for bit in bits_of("gc")[1:]:
            grads.update({m | bit: swap(v, "gc", bit) for m, v in list(grads.items())})
        held.update({m + 1: swap(held[m], "gr", 1) for m in [first, 2, *others]})
        values = block_values[0, 0]
        info = pl.pallas_call(
            info_kernel,
            out_shape=jax.ShapeDtypeStruct((8, 128 * pl.cdiv(values.shape[0], 128)), jnp.int32),
            in_specs=[VMEM] * 3,
            out_specs=VMEM,
            compiler_params=params(limit),
            cost_estimate=pl.CostEstimate(flops=5 * 10**9, bytes_accessed=0, transcendentals=0),
        )(*[after(v, held[2]) for v in (block_rows[0], block_cols[0], block_counts)])
    layout = [(m,) for m in held]
    held[0] = after(x, *grads.values())
    pieces = list(held.values())

    with jax.named_scope("forward_blocks"):
        send_masks = [m for m in range(gc_size) if m & 1]
        keep_masks = [m for m in range(gc_size) if not m & 1]
        send, keep = pl.pallas_call(
            functools.partial(forward_kernel, layout, send_masks, keep_masks),
            out_shape=[stacked(len(send_masks)), stacked(len(keep_masks))],
            in_specs=[SMEM] + [VMEM] * (1 + len(pieces)),
            out_specs=[VMEM, VMEM],
            scratch_shapes=[
                pltpu.VMEM((gr_size, side, width), jnp.bfloat16),
                pltpu.VMEM((gc_size, side, width), jnp.float32),
            ],
            compiler_params=params(limit),
        )(info, values, *pieces)

    with jax.named_scope("sum_rows"):
        near = swap(send, "gc", 1)
        mine = bf16(f32(keep) + f32(near))
        *bits, last = bits_of("gc")[1:]
        for bit in bits:
            order = jnp.arange(len(keep_masks)) ^ (bit >> 1)
            got = swap(mine, "gc", bit).reshape(-1, side, width)[order].reshape(mine.shape)
            mine = bf16(f32(mine) + f32(got))
        got = swap(mine, "gc", last)

    half = width // 2
    with jax.named_scope("dense"):
        activated, message, kept = pl.pallas_call(
            functools.partial(dense_kernel, last >> 1),
            out_shape=[
                block,
                jax.ShapeDtypeStruct((mine.shape[0] + half, width), jnp.bfloat16),
                jax.ShapeDtypeStruct((half, width), jnp.float32),
            ],
            in_specs=[VMEM] * (3 + len(grads)),
            out_specs=[VMEM] * 3,
            scratch_shapes=[pltpu.VMEM((width, width), jnp.float32)],
            compiler_params=params(limit),
        )(mine, got, weight, *[grads[m] for m in keep_masks])

    with jax.named_scope("swap_cores"):
        answer = swap(message, "gc", 1)
        running = kept + f32(answer[mine.shape[0]:])
    stages = bits_of("gr")[:0:-1] + [1]
    sent, got, order = [], [], Line()

    def launch(running):
        with jax.named_scope("sum_weight"):
            sent.append(bf16(running))
            got.append(swap_crossed(sent[-1], stages[len(sent) - 1]))

    def advance():
        if len(sent) > len(stages):
            return
        with jax.named_scope("sum_weight"):
            running = f32(sent[-1]) + f32(order(got[-1]))
            if len(sent) < len(stages):
                launch(running)
            else:
                sent.append(bf16(running))
                got.append(swap(sent[-1], "gc", 1))

    launch(running)

    with jax.named_scope("backward_blocks"):
        kept_masks = [(m,) for m in far_first[:-1]] + [(2, 0)]
        out_layout = [tuple(m + 1 for m in masks) for masks in kept_masks] + kept_masks
        outs = pl.pallas_call(
            functools.partial(backward_kernel, [keep_masks, send_masks], out_layout),
            out_shape=[stacked(len(masks)) for masks in out_layout],
            in_specs=[SMEM] + [VMEM] * 3,
            out_specs=[VMEM] * len(out_layout),
            scratch_shapes=[
                pltpu.VMEM((gc_size, side, width), jnp.bfloat16),
                pltpu.VMEM((gr_size, side, width), jnp.float32),
            ],
            compiler_params=params(limit),
        )(info, values, message, answer)
        sends, keeps = outs[: len(kept_masks)], outs[len(kept_masks):]

    with jax.named_scope("sum_columns"):
        arrived = [swap(v, "gr", 1) for v in sends]
        order(keeps[0])
        advance()
        parts = []
        for masks, kept, part in zip(kept_masks[:-1], keeps, arrived):
            total = bf16(f32(kept) + f32(order(part)))
            parts += [(m, total[n * side : (n + 1) * side]) for n, m in enumerate(masks)]
        terms = [swap(v, "gr", m) for m, v in parts]
        own = (keeps[-1], order(arrived[-1]))
        total = bf16(f32(own[0][:side]) + f32(own[1][:side]))
        terms.append(swap(total, "gr", 2))
        advance()
    while len(sent) <= len(stages):
        advance()
    terms = [order(term) for term in terms]
    running, other = sent[-1], order(got[-1])

    grad_features, grad_weight = pl.pallas_call(
        finish_kernel,
        out_shape=[
            jax.ShapeDtypeStruct((side, width), jnp.float32),
            jax.ShapeDtypeStruct((width, width), jnp.float32),
        ],
        in_specs=[VMEM] * (4 + len(terms)),
        out_specs=[VMEM] * 2,
        compiler_params=params(limit),
    )(running, other, *own, *terms)
    return activated[None], grad_weight, grad_features[None]


def solution(mesh):
    placed = (
        P("gc", "gr", None),
        P(),
        P("gr", "gc", None),
        P("gr", "gc", None),
        P("gr", "gc", None),
        P("gr", "gc"),
        P("gr", "gc", None, None, None),
    )
    return jax.shard_map(
        per_device,
        mesh=mesh,
        in_specs=placed,
        out_specs=(P("gr", "gc", None), P(), P("gc", "gr", None)),
        check_vma=False,
    )
```

```python
import functools

import jax
import jax.numpy as jnp
from jax import lax
from jax.experimental import pallas as pl
from jax.experimental.pallas import tpu as pltpu
from jax.sharding import PartitionSpec as P

VMEM = pl.BlockSpec(memory_space=pltpu.VMEM)
SMEM = pl.BlockSpec(memory_space=pltpu.SMEM)
FULL = (((1,), (0,)), ((), ()))
LEFT_T = (((0,), (0,)), ((), ()))
RIGHT_T = (((1,), (1,)), ((), ()))


def f32(value):
    return value.astype(jnp.float32)


def bf16(value):
    return value.astype(jnp.bfloat16)


def swap(value, axis, mask):
    size = lax.axis_size(axis)
    return lax.ppermute(value, axis, [(i, i ^ mask) for i in range(size)])


def swap_crossed(value, mask):
    rows, cols = lax.axis_size("gr"), lax.axis_size("gc")
    pairs = [
        (r * cols + c, (r ^ mask) * cols + (c ^ 1)) for r in range(rows) for c in range(cols)
    ]
    return lax.ppermute(value, ("gr", "gc"), pairs)


def weight_half():
    half, rows = lax.axis_index("gc"), lax.axis_index("gr")
    for b in range(lax.axis_size("gr").bit_length() - 1):
        half = half ^ (rows >> b)
    return half & 1


def bits_of(axis):
    return [1 << b for b in range(lax.axis_size(axis).bit_length() - 1)]


def after(value, *deps):
    return lax.optimization_barrier((value, *deps))[0]


class Line:
    def __init__(self):
        self.last = None

    def __call__(self, value):
        self.last = value if self.last is None else after(value, self.last)
        return self.last


def params(nbytes):
    return pltpu.CompilerParams(vmem_limit_bytes=nbytes)


def slot_products(transposed, info, values, source, total):
    slots = values.shape[0]
    count = info[2, 0]
    dims = LEFT_T if transposed else FULL

    def place(s):
        row, col = info[0, s], info[1, s]
        return (row, col) if transposed else (col, row)

    def product(s):
        return lax.dot_general(
            values[s], source[place(s)[0]], dims, preferred_element_type=jnp.float32
        )

    total[...] = jnp.zeros_like(total)
    if slots <= 8:
        products = [product(s) for s in range(slots)]
        for s in range(slots):
            total[place(s)[1]] += jnp.where(s < count, products[s], 0.0)
    else:

        def one(s, _):
            total[place(s)[1]] += product(s)
            return 0

        lax.fori_loop(0, count, one, 0)


def info_kernel(rows, cols, counts, info):
    slots = rows.shape[1]
    info[...] = jnp.zeros_like(info)
    info[0:1, pl.ds(0, slots)] = rows[...] ^ lax.axis_index("gc")
    info[1:2, pl.ds(0, slots)] = cols[...] ^ lax.axis_index("gr")
    info[2:3, pl.ds(0, 1)] = counts[...]


def forward_kernel(layout, send_masks, keep_masks, info, values, *refs):
    pieces, (send, keep, source, total) = refs[: len(layout)], refs[len(layout):]
    side = values.shape[1]
    for masks, piece in zip(layout, pieces):
        for n, m in enumerate(masks):
            source[m] = piece[pl.ds(n * side, side), :]
    slot_products(False, info, values, source, total)
    for n, m in enumerate(send_masks):
        send[pl.ds(n * side, side), :] = bf16(total[m])
    for n, m in enumerate(keep_masks):
        keep[pl.ds(n * side, side), :] = bf16(total[m])


def backward_kernel(layout, out_layout, info, values, *refs):
    pieces, rest = refs[: len(layout)], refs[len(layout):]
    outs, (source, total) = rest[: len(out_layout)], rest[len(out_layout):]
    side = values.shape[1]
    for masks, piece in zip(layout, pieces):
        for n, m in enumerate(masks):
            source[m] = piece[pl.ds(n * side, side), :]
    slot_products(True, info, values, source, total)
    for masks, out in zip(out_layout, outs):
        for n, m in enumerate(masks):
            out[pl.ds(n * side, side), :] = bf16(total[m])


def dense_kernel(bit, mine, got, weight, *refs):
    *grads, activated, message, kept, total = refs
    side, half = activated.shape[0], kept.shape[0]
    blocks = mine.shape[0] // side
    w = weight[...]
    summed = [
        f32(mine[pl.ds(e * side, side), :]) + f32(got[pl.ds((e ^ bit) * side, side), :])
        for e in range(blocks)
    ]
    hidden = bf16(jnp.concatenate(summed))
    pre = lax.dot_general(hidden, w, FULL, preferred_element_type=jnp.float32)
    s = 1.0 / (1.0 + jnp.exp(-pre))
    activated[...] = bf16(pre[:side] * s[:side])
    grad_out = jnp.concatenate([f32(g[...]) for g in grads])
    grad_pre = bf16(grad_out * s * (1.0 + pre * (1.0 - s)))
    message[pl.ds(0, blocks * side), :] = bf16(
        lax.dot_general(grad_pre, w, RIGHT_T, preferred_element_type=jnp.float32)
    )
    total[...] = lax.dot_general(hidden, grad_pre, LEFT_T, preferred_element_type=jnp.float32)
    place = weight_half()
    kept[...] = total[pl.ds(pl.multiple_of(place * half, half), half), :]
    message[pl.ds(blocks * side, half), :] = bf16(
        total[pl.ds(pl.multiple_of((1 - place) * half, half), half), :]
    )


def finish_kernel(mine, other, *refs):
    (kept, part, *terms), (grad_features, grad_weight) = refs[:-2], refs[-2:]
    side = grad_features.shape[0]
    parts = [f32(v[pl.ds(side, side), :]) for v in (kept, part)] + [f32(t[...]) for t in terms]
    grad_features[...] = functools.reduce(lambda a, b: a + b, parts)
    half = mine.shape[0]
    place = weight_half()
    grad_weight[pl.ds(pl.multiple_of(place * half, half), half), :] = f32(mine[...])
    grad_weight[pl.ds(pl.multiple_of((1 - place) * half, half), half), :] = f32(other[...])


def per_device(features, weight, grad_out, block_rows, block_cols, block_counts, block_values):
    side, width = features.shape[1:]
    gr_size, gc_size = lax.axis_size("gr"), lax.axis_size("gc")
    outer = [m for m in range(0, gr_size, 2)]
    far_first = sorted(outer[2:]) + [2]
    block = jax.ShapeDtypeStruct((side, width), jnp.bfloat16)

    def stacked(n):
        return jax.ShapeDtypeStruct((n * side, width), jnp.bfloat16)

    limit = 48 * 2**20
    with jax.named_scope("gather_features"):
        x = features[0]
        first, *others = far_first[:-1]
        held = {m: swap(x, "gr", m) for m in [1, first, 2, *others]}
        held[0] = x
        grads = {0: after(grad_out[0], held[2])}
        for bit in bits_of("gc")[1:]:
            grads.update({m | bit: swap(v, "gc", bit) for m, v in list(grads.items())})
        held.update({m + 1: swap(held[m], "gr", 1) for m in [first, 2, *others]})
        values = block_values[0, 0]
        info = pl.pallas_call(
            info_kernel,
            out_shape=jax.ShapeDtypeStruct((8, 128 * pl.cdiv(values.shape[0], 128)), jnp.int32),
            in_specs=[VMEM] * 3,
            out_specs=VMEM,
            compiler_params=params(limit),
            cost_estimate=pl.CostEstimate(flops=5 * 10**9, bytes_accessed=0, transcendentals=0),
        )(*[after(v, held[2]) for v in (block_rows[0], block_cols[0], block_counts)])
    layout = [(m,) for m in held]
    held[0] = after(x, *grads.values())
    pieces = list(held.values())

    with jax.named_scope("forward_blocks"):
        send_masks = [m for m in range(gc_size) if m & 1]
        keep_masks = [m for m in range(gc_size) if not m & 1]
        send, keep = pl.pallas_call(
            functools.partial(forward_kernel, layout, send_masks, keep_masks),
            out_shape=[stacked(len(send_masks)), stacked(len(keep_masks))],
            in_specs=[SMEM] + [VMEM] * (1 + len(pieces)),
            out_specs=[VMEM, VMEM],
            scratch_shapes=[
                pltpu.VMEM((gr_size, side, width), jnp.bfloat16),
                pltpu.VMEM((gc_size, side, width), jnp.float32),
            ],
            compiler_params=params(limit),
        )(info, values, *pieces)

    with jax.named_scope("sum_rows"):
        near = swap(send, "gc", 1)
        mine = bf16(f32(keep) + f32(near))
        *bits, last = bits_of("gc")[1:]
        for bit in bits:
            order = jnp.arange(len(keep_masks)) ^ (bit >> 1)
            got = swap(mine, "gc", bit).reshape(-1, side, width)[order].reshape(mine.shape)
            mine = bf16(f32(mine) + f32(got))
        got = swap(mine, "gc", last)

    half = width // 2
    with jax.named_scope("dense"):
        activated, message, kept = pl.pallas_call(
            functools.partial(dense_kernel, last >> 1),
            out_shape=[
                block,
                jax.ShapeDtypeStruct((mine.shape[0] + half, width), jnp.bfloat16),
                jax.ShapeDtypeStruct((half, width), jnp.float32),
            ],
            in_specs=[VMEM] * (3 + len(grads)),
            out_specs=[VMEM] * 3,
            scratch_shapes=[pltpu.VMEM((width, width), jnp.float32)],
            compiler_params=params(limit),
        )(mine, got, weight, *[grads[m] for m in keep_masks])

    with jax.named_scope("swap_cores"):
        answer = swap(message, "gc", 1)
        running = kept + f32(answer[mine.shape[0]:])
    stages = bits_of("gr")[:0:-1] + [1]
    sent, got, order = [], [], Line()

    def launch(running):
        with jax.named_scope("sum_weight"):
            sent.append(bf16(running))
            got.append(swap_crossed(sent[-1], stages[len(sent) - 1]))

    def advance():
        if len(sent) > len(stages):
            return
        with jax.named_scope("sum_weight"):
            running = f32(sent[-1]) + f32(order(got[-1]))
            if len(sent) < len(stages):
                launch(running)
            else:
                sent.append(bf16(running))
                got.append(swap(sent[-1], "gc", 1))

    launch(running)

    with jax.named_scope("backward_blocks"):
        kept_masks = [(m,) for m in far_first[:-1]] + [(2, 0)]
        out_layout = [tuple(m + 1 for m in masks) for masks in kept_masks] + kept_masks
        outs = pl.pallas_call(
            functools.partial(backward_kernel, [keep_masks, send_masks], out_layout),
            out_shape=[stacked(len(masks)) for masks in out_layout],
            in_specs=[SMEM] + [VMEM] * 3,
            out_specs=[VMEM] * len(out_layout),
            scratch_shapes=[
                pltpu.VMEM((gc_size, side, width), jnp.bfloat16),
                pltpu.VMEM((gr_size, side, width), jnp.float32),
            ],
            compiler_params=params(limit),
        )(info, values, message, answer)
        sends, keeps = outs[: len(kept_masks)], outs[len(kept_masks):]

    with jax.named_scope("sum_columns"):
        arrived = [swap(v, "gr", 1) for v in sends]
        order(keeps[0])
        advance()
        parts = []
        for masks, kept, part in zip(kept_masks[:-1], keeps, arrived):
            total = bf16(f32(kept) + f32(order(part)))
            parts += [(m, total[n * side : (n + 1) * side]) for n, m in enumerate(masks)]
        terms = [swap(v, "gr", m) for m, v in parts]
        own = (keeps[-1], order(arrived[-1]))
        total = bf16(f32(own[0][:side]) + f32(own[1][:side]))
        terms.append(swap(total, "gr", 2))
        advance()
    while len(sent) <= len(stages):
        advance()
    terms = [order(term) for term in terms]
    running, other = sent[-1], order(got[-1])

    grad_features, grad_weight = pl.pallas_call(
        finish_kernel,
        out_shape=[
            jax.ShapeDtypeStruct((side, width), jnp.float32),
            jax.ShapeDtypeStruct((width, width), jnp.float32),
        ],
        in_specs=[VMEM] * (4 + len(terms)),
        out_specs=[VMEM] * 2,
        compiler_params=params(limit),
    )(running, other, *own, *terms)
    return activated[None], grad_weight, grad_features[None]


def solution(mesh):
    placed = (
        P("gc", "gr", None),
        P(),
        P("gr", "gc", None),
        P("gr", "gc", None),
        P("gr", "gc", None),
        P("gr", "gc"),
        P("gr", "gc", None, None, None),
    )
    return jax.shard_map(
        per_device,
        mesh=mesh,
        in_specs=placed,
        out_specs=(P("gr", "gc", None), P(), P("gc", "gr", None)),
        check_vma=False,
    )
```

```python
import functools

import jax
import jax.numpy as jnp
from jax import lax
from jax.experimental import pallas as pl
from jax.experimental.pallas import tpu as pltpu
from jax.sharding import PartitionSpec as P

VMEM = pl.BlockSpec(memory_space=pltpu.VMEM)
SMEM = pl.BlockSpec(memory_space=pltpu.SMEM)
FULL = (((1,), (0,)), ((), ()))
LEFT_T = (((0,), (0,)), ((), ()))
RIGHT_T = (((1,), (1,)), ((), ()))


def f32(value):
    return value.astype(jnp.float32)


def bf16(value):
    return value.astype(jnp.bfloat16)


def swap(value, axis, mask):
    size = lax.axis_size(axis)
    return lax.ppermute(value, axis, [(i, i ^ mask) for i in range(size)])


def swap_crossed(value, mask):
    rows, cols = lax.axis_size("gr"), lax.axis_size("gc")
    pairs = [
        (r * cols + c, (r ^ mask) * cols + (c ^ 1)) for r in range(rows) for c in range(cols)
    ]
    return lax.ppermute(value, ("gr", "gc"), pairs)


def weight_half():
    half, rows = lax.axis_index("gc"), lax.axis_index("gr")
    for b in range(lax.axis_size("gr").bit_length() - 1):
        half = half ^ (rows >> b)
    return half & 1


def bits_of(axis):
    return [1 << b for b in range(lax.axis_size(axis).bit_length() - 1)]


def after(value, *deps):
    return lax.optimization_barrier((value, *deps))[0]


class Line:
    def __init__(self):
        self.last = None

    def __call__(self, value):
        self.last = value if self.last is None else after(value, self.last)
        return self.last


def params(nbytes):
    return pltpu.CompilerParams(vmem_limit_bytes=nbytes)


def slot_products(transposed, info, values, source, total):
    slots = values.shape[0]
    count = info[2, 0]
    dims = LEFT_T if transposed else FULL

    def place(s):
        row, col = info[0, s], info[1, s]
        return (row, col) if transposed else (col, row)

    def product(s):
        return lax.dot_general(
            values[s], source[place(s)[0]], dims, preferred_element_type=jnp.float32
        )

    total[...] = jnp.zeros_like(total)
    if slots <= 8:
        products = [product(s) for s in range(slots)]
        for s in range(slots):
            total[place(s)[1]] += jnp.where(s < count, products[s], 0.0)
    else:

        def one(s, _):
            total[place(s)[1]] += product(s)
            return 0

        lax.fori_loop(0, count, one, 0)


def info_kernel(rows, cols, counts, info):
    slots = rows.shape[1]
    info[...] = jnp.zeros_like(info)
    info[0:1, pl.ds(0, slots)] = rows[...] ^ lax.axis_index("gc")
    info[1:2, pl.ds(0, slots)] = cols[...] ^ lax.axis_index("gr")
    info[2:3, pl.ds(0, 1)] = counts[...]


def forward_kernel(layout, send_masks, keep_masks, info, values, *refs):
    pieces, (send, keep, source, total) = refs[: len(layout)], refs[len(layout):]
    side = values.shape[1]
    for masks, piece in zip(layout, pieces):
        for n, m in enumerate(masks):
            source[m] = piece[pl.ds(n * side, side), :]
    slot_products(False, info, values, source, total)
    for n, m in enumerate(send_masks):
        send[pl.ds(n * side, side), :] = bf16(total[m])
    for n, m in enumerate(keep_masks):
        keep[pl.ds(n * side, side), :] = bf16(total[m])


def backward_kernel(layout, out_layout, info, values, *refs):
    pieces, rest = refs[: len(layout)], refs[len(layout):]
    outs, (source, total) = rest[: len(out_layout)], rest[len(out_layout):]
    side = values.shape[1]
    for masks, piece in zip(layout, pieces):
        for n, m in enumerate(masks):
            source[m] = piece[pl.ds(n * side, side), :]
    slot_products(True, info, values, source, total)
    for masks, out in zip(out_layout, outs):
        for n, m in enumerate(masks):
            out[pl.ds(n * side, side), :] = bf16(total[m])


def dense_kernel(bit, mine, got, weight, *refs):
    *grads, activated, message, passed, kept, total = refs
    side, half = activated.shape[0], kept.shape[0]
    blocks = mine.shape[0] // side
    w = weight[...]
    summed = [
        f32(mine[pl.ds(e * side, side), :]) + f32(got[pl.ds((e ^ bit) * side, side), :])
        for e in range(blocks)
    ]
    hidden = bf16(jnp.concatenate(summed))
    pre = lax.dot_general(hidden, w, FULL, preferred_element_type=jnp.float32)
    s = 1.0 / (1.0 + jnp.exp(-pre))
    activated[...] = bf16(pre[:side] * s[:side])
    grad_out = jnp.concatenate([f32(g[...]) for g in grads])
    grad_pre = bf16(grad_out * s * (1.0 + pre * (1.0 - s)))
    message[pl.ds(0, blocks * side), :] = bf16(
        lax.dot_general(grad_pre, w, RIGHT_T, preferred_element_type=jnp.float32)
    )
    total[...] = lax.dot_general(hidden, grad_pre, LEFT_T, preferred_element_type=jnp.float32)
    place = weight_half()
    kept[...] = total[pl.ds(pl.multiple_of(place * half, half), half), :]
    passed[...] = bf16(
        total[pl.ds(pl.multiple_of((1 - place) * half, half), half), :]
    )


def finish_kernel(mine, other, *refs):
    (kept, part, *terms), (grad_features, grad_weight) = refs[:-2], refs[-2:]
    side = grad_features.shape[0]
    parts = [f32(v[pl.ds(side, side), :]) for v in (kept, part)] + [f32(t[...]) for t in terms]
    grad_features[...] = functools.reduce(lambda a, b: a + b, parts)
    half = mine.shape[0]
    place = weight_half()
    grad_weight[pl.ds(pl.multiple_of(place * half, half), half), :] = f32(mine[...])
    grad_weight[pl.ds(pl.multiple_of((1 - place) * half, half), half), :] = f32(other[...])


def per_device(features, weight, grad_out, block_rows, block_cols, block_counts, block_values):
    side, width = features.shape[1:]
    gr_size, gc_size = lax.axis_size("gr"), lax.axis_size("gc")
    outer = [m for m in range(0, gr_size, 2)]
    far_first = sorted(outer[2:]) + [2]
    block = jax.ShapeDtypeStruct((side, width), jnp.bfloat16)

    def stacked(n):
        return jax.ShapeDtypeStruct((n * side, width), jnp.bfloat16)

    limit = 48 * 2**20
    with jax.named_scope("gather_features"):
        x = features[0]
        first, *others = far_first[:-1]
        held = {m: swap(x, "gr", m) for m in [1, first, 2, *others]}
        held[0] = x
        grads = {0: after(grad_out[0], held[2])}
        for bit in bits_of("gc")[1:]:
            grads.update({m | bit: swap(v, "gc", bit) for m, v in list(grads.items())})
        held.update({m + 1: swap(held[m], "gr", 1) for m in [first, 2, *others]})
        values = block_values[0, 0]
        info = pl.pallas_call(
            info_kernel,
            out_shape=jax.ShapeDtypeStruct((8, 128 * pl.cdiv(values.shape[0], 128)), jnp.int32),
            in_specs=[VMEM] * 3,
            out_specs=VMEM,
            compiler_params=params(limit),
            cost_estimate=pl.CostEstimate(flops=5 * 10**9, bytes_accessed=0, transcendentals=0),
        )(*[after(v, held[2]) for v in (block_rows[0], block_cols[0], block_counts)])
    layout = [(m,) for m in held]
    held[0] = after(x, *grads.values())
    pieces = list(held.values())

    with jax.named_scope("forward_blocks"):
        send_masks = [m for m in range(gc_size) if m & 1]
        keep_masks = [m for m in range(gc_size) if not m & 1]
        send, keep = pl.pallas_call(
            functools.partial(forward_kernel, layout, send_masks, keep_masks),
            out_shape=[stacked(len(send_masks)), stacked(len(keep_masks))],
            in_specs=[SMEM] + [VMEM] * (1 + len(pieces)),
            out_specs=[VMEM, VMEM],
            scratch_shapes=[
                pltpu.VMEM((gr_size, side, width), jnp.bfloat16),
                pltpu.VMEM((gc_size, side, width), jnp.float32),
            ],
            compiler_params=params(limit),
        )(info, values, *pieces)

    with jax.named_scope("sum_rows"):
        near = swap(send, "gc", 1)
        mine = bf16(f32(keep) + f32(near))
        *bits, last = bits_of("gc")[1:]
        for bit in bits:
            order = jnp.arange(len(keep_masks)) ^ (bit >> 1)
            got = swap(mine, "gc", bit).reshape(-1, side, width)[order].reshape(mine.shape)
            mine = bf16(f32(mine) + f32(got))
        got = swap(mine, "gc", last)

    half = width // 2
    with jax.named_scope("dense"):
        activated, message, passed, kept = pl.pallas_call(
            functools.partial(dense_kernel, last >> 1),
            out_shape=[
                block,
                jax.ShapeDtypeStruct(mine.shape, jnp.bfloat16),
                jax.ShapeDtypeStruct((half, width), jnp.bfloat16),
                jax.ShapeDtypeStruct((half, width), jnp.float32),
            ],
            in_specs=[VMEM] * (3 + len(grads)),
            out_specs=[VMEM] * 4,
            scratch_shapes=[pltpu.VMEM((width, width), jnp.float32)],
            compiler_params=params(limit),
        )(mine, got, weight, *[grads[m] for m in keep_masks])

    with jax.named_scope("swap_cores"):
        answer = swap(message, "gc", 1)
        passed = swap(passed, "gc", 1)
        running = kept + f32(after(passed, answer))
    stages = bits_of("gr")[:0:-1] + [1]
    sent, got, order = [], [], Line()

    def launch(running):
        with jax.named_scope("sum_weight"):
            sent.append(bf16(running))
            got.append(swap_crossed(sent[-1], stages[len(sent) - 1]))

    def advance():
        if len(sent) > len(stages):
            return
        with jax.named_scope("sum_weight"):
            running = f32(sent[-1]) + f32(order(got[-1]))
            if len(sent) < len(stages):
                launch(running)
            else:
                sent.append(bf16(running))
                got.append(swap(sent[-1], "gc", 1))

    launch(running)

    with jax.named_scope("backward_blocks"):
        kept_masks = [(m,) for m in far_first[:-1]] + [(2, 0)]
        out_layout = [tuple(m + 1 for m in masks) for masks in kept_masks] + kept_masks
        outs = pl.pallas_call(
            functools.partial(backward_kernel, [keep_masks, send_masks], out_layout),
            out_shape=[stacked(len(masks)) for masks in out_layout],
            in_specs=[SMEM] + [VMEM] * 3,
            out_specs=[VMEM] * len(out_layout),
            scratch_shapes=[
                pltpu.VMEM((gc_size, side, width), jnp.bfloat16),
                pltpu.VMEM((gr_size, side, width), jnp.float32),
            ],
            compiler_params=params(limit),
        )(info, values, message, answer)
        sends, keeps = outs[: len(kept_masks)], outs[len(kept_masks):]

    with jax.named_scope("sum_columns"):
        arrived = [swap(v, "gr", 1) for v in sends]
        order(keeps[0])
        advance()
        parts = []
        for masks, kept, part in zip(kept_masks[:-1], keeps, arrived):
            total = bf16(f32(kept) + f32(order(part)))
            parts += [(m, total[n * side : (n + 1) * side]) for n, m in enumerate(masks)]
        terms = [swap(v, "gr", m) for m, v in parts]
        own = (keeps[-1], order(arrived[-1]))
        total = bf16(f32(own[0][:side]) + f32(own[1][:side]))
        terms.append(swap(total, "gr", 2))
        advance()
    while len(sent) <= len(stages):
        advance()
    terms = [order(term) for term in terms]
    running, other = sent[-1], order(got[-1])

    grad_features, grad_weight = pl.pallas_call(
        finish_kernel,
        out_shape=[
            jax.ShapeDtypeStruct((side, width), jnp.float32),
            jax.ShapeDtypeStruct((width, width), jnp.float32),
        ],
        in_specs=[VMEM] * (4 + len(terms)),
        out_specs=[VMEM] * 2,
        compiler_params=params(limit),
    )(running, other, *own, *terms)
    return activated[None], grad_weight, grad_features[None]


def solution(mesh):
    placed = (
        P("gc", "gr", None),
        P(),
        P("gr", "gc", None),
        P("gr", "gc", None),
        P("gr", "gc", None),
        P("gr", "gc"),
        P("gr", "gc", None, None, None),
    )
    return jax.shard_map(
        per_device,
        mesh=mesh,
        in_specs=placed,
        out_specs=(P("gr", "gc", None), P(), P("gc", "gr", None)),
        check_vma=False,
    )
```

```python
import functools

import jax
import jax.numpy as jnp
from jax import lax
from jax.experimental import pallas as pl
from jax.experimental.pallas import tpu as pltpu
from jax.sharding import PartitionSpec as P

VMEM = pl.BlockSpec(memory_space=pltpu.VMEM)
SMEM = pl.BlockSpec(memory_space=pltpu.SMEM)
FULL = (((1,), (0,)), ((), ()))
LEFT_T = (((0,), (0,)), ((), ()))
RIGHT_T = (((1,), (1,)), ((), ()))


def f32(value):
    return value.astype(jnp.float32)


def bf16(value):
    return value.astype(jnp.bfloat16)


def swap(value, axis, mask):
    size = lax.axis_size(axis)
    return lax.ppermute(value, axis, [(i, i ^ mask) for i in range(size)])


def swap_crossed(value, mask):
    rows, cols = lax.axis_size("gr"), lax.axis_size("gc")
    pairs = [
        (r * cols + c, (r ^ mask) * cols + (c ^ 1)) for r in range(rows) for c in range(cols)
    ]
    return lax.ppermute(value, ("gr", "gc"), pairs)


def weight_half():
    half, rows = lax.axis_index("gc"), lax.axis_index("gr")
    for b in range(lax.axis_size("gr").bit_length() - 1):
        half = half ^ (rows >> b)
    return half & 1


def bits_of(axis):
    return [1 << b for b in range(lax.axis_size(axis).bit_length() - 1)]


def after(value, *deps):
    return lax.optimization_barrier((value, *deps))[0]


class Line:
    def __init__(self):
        self.last = None

    def __call__(self, value):
        self.last = value if self.last is None else after(value, self.last)
        return self.last


def params(nbytes):
    return pltpu.CompilerParams(vmem_limit_bytes=nbytes)


def slot_products(transposed, info, values, source, total):
    slots = values.shape[0]
    count = info[2, 0]
    dims = LEFT_T if transposed else FULL

    def place(s):
        row, col = info[0, s], info[1, s]
        return (row, col) if transposed else (col, row)

    def product(s):
        return lax.dot_general(
            values[s], source[place(s)[0]], dims, preferred_element_type=jnp.float32
        )

    total[...] = jnp.zeros_like(total)
    if slots <= 8:
        products = [product(s) for s in range(slots)]
        for s in range(slots):
            total[place(s)[1]] += jnp.where(s < count, products[s], 0.0)
    else:

        def one(s, _):
            total[place(s)[1]] += product(s)
            return 0

        lax.fori_loop(0, count, one, 0)


def info_kernel(rows, cols, counts, info):
    gr, gc = lax.axis_index("gr"), lax.axis_index("gc")

    def one(s, _):
        info[0, s] = rows[0, s] ^ gc
        info[1, s] = cols[0, s] ^ gr
        return 0

    lax.fori_loop(0, rows.shape[1], one, 0)
    info[2, 0] = counts[0, 0]


def forward_kernel(layout, send_masks, keep_masks, info, values, *refs):
    pieces, (send, keep, source, total) = refs[: len(layout)], refs[len(layout):]
    side = values.shape[1]
    for masks, piece in zip(layout, pieces):
        for n, m in enumerate(masks):
            source[m] = piece[pl.ds(n * side, side), :]
    slot_products(False, info, values, source, total)
    for n, m in enumerate(send_masks):
        send[pl.ds(n * side, side), :] = bf16(total[m])
    for n, m in enumerate(keep_masks):
        keep[pl.ds(n * side, side), :] = bf16(total[m])


def backward_kernel(layout, out_layout, info, values, *refs):
    pieces, rest = refs[: len(layout)], refs[len(layout):]
    outs, (source, total) = rest[: len(out_layout)], rest[len(out_layout):]
    side = values.shape[1]
    for masks, piece in zip(layout, pieces):
        for n, m in enumerate(masks):
            source[m] = piece[pl.ds(n * side, side), :]
    slot_products(True, info, values, source, total)
    for masks, out in zip(out_layout, outs):
        for n, m in enumerate(masks):
            out[pl.ds(n * side, side), :] = bf16(total[m])


def dense_kernel(bit, mine, got, weight, *refs):
    *grads, activated, message, passed, kept, total = refs
    side, half = activated.shape[0], kept.shape[0]
    blocks = mine.shape[0] // side
    w = weight[...]
    summed = [
        f32(mine[pl.ds(e * side, side), :]) + f32(got[pl.ds((e ^ bit) * side, side), :])
        for e in range(blocks)
    ]
    hidden = bf16(jnp.concatenate(summed))
    pre = lax.dot_general(hidden, w, FULL, preferred_element_type=jnp.float32)
    s = 1.0 / (1.0 + jnp.exp(-pre))
    activated[...] = bf16(pre[:side] * s[:side])
    grad_out = jnp.concatenate([f32(g[...]) for g in grads])
    grad_pre = bf16(grad_out * s * (1.0 + pre * (1.0 - s)))
    message[pl.ds(0, blocks * side), :] = bf16(
        lax.dot_general(grad_pre, w, RIGHT_T, preferred_element_type=jnp.float32)
    )
    total[...] = lax.dot_general(hidden, grad_pre, LEFT_T, preferred_element_type=jnp.float32)
    place = weight_half()
    kept[...] = total[pl.ds(pl.multiple_of(place * half, half), half), :]
    passed[...] = bf16(
        total[pl.ds(pl.multiple_of((1 - place) * half, half), half), :]
    )


def finish_kernel(mine, other, *refs):
    (kept, part, *terms), (grad_features, grad_weight) = refs[:-2], refs[-2:]
    side = grad_features.shape[0]
    parts = [f32(v[pl.ds(side, side), :]) for v in (kept, part)] + [f32(t[...]) for t in terms]
    grad_features[...] = functools.reduce(lambda a, b: a + b, parts)
    half = mine.shape[0]
    place = weight_half()
    grad_weight[pl.ds(pl.multiple_of(place * half, half), half), :] = f32(mine[...])
    grad_weight[pl.ds(pl.multiple_of((1 - place) * half, half), half), :] = f32(other[...])


def per_device(features, weight, grad_out, block_rows, block_cols, block_counts, block_values):
    side, width = features.shape[1:]
    gr_size, gc_size = lax.axis_size("gr"), lax.axis_size("gc")
    outer = [m for m in range(0, gr_size, 2)]
    far_first = sorted(outer[2:]) + [2]
    block = jax.ShapeDtypeStruct((side, width), jnp.bfloat16)

    def stacked(n):
        return jax.ShapeDtypeStruct((n * side, width), jnp.bfloat16)

    limit = 48 * 2**20
    with jax.named_scope("gather_features"):
        x = features[0]
        first, *others = far_first[:-1]
        held = {m: swap(x, "gr", m) for m in [1, first, 2, *others]}
        held[0] = x
        grads = {0: after(grad_out[0], held[2])}
        for bit in bits_of("gc")[1:]:
            grads.update({m | bit: swap(v, "gc", bit) for m, v in list(grads.items())})
        held.update({m + 1: swap(held[m], "gr", 1) for m in [first, 2, *others]})
        values = block_values[0, 0]
        info = pl.pallas_call(
            info_kernel,
            out_shape=jax.ShapeDtypeStruct((3, values.shape[0]), jnp.int32),
            in_specs=[SMEM] * 3,
            out_specs=SMEM,
            compiler_params=params(limit),
            cost_estimate=pl.CostEstimate(flops=5 * 10**9, bytes_accessed=0, transcendentals=0),
        )(*[after(v, held[2]) for v in (block_rows[0], block_cols[0], block_counts)])
    layout = [(m,) for m in held]
    held[0] = after(x, *grads.values())
    pieces = list(held.values())

    with jax.named_scope("forward_blocks"):
        send_masks = [m for m in range(gc_size) if m & 1]
        keep_masks = [m for m in range(gc_size) if not m & 1]
        send, keep = pl.pallas_call(
            functools.partial(forward_kernel, layout, send_masks, keep_masks),
            out_shape=[stacked(len(send_masks)), stacked(len(keep_masks))],
            in_specs=[SMEM] + [VMEM] * (1 + len(pieces)),
            out_specs=[VMEM, VMEM],
            scratch_shapes=[
                pltpu.VMEM((gr_size, side, width), jnp.bfloat16),
                pltpu.VMEM((gc_size, side, width), jnp.float32),
            ],
            compiler_params=params(limit),
        )(info, values, *pieces)

    with jax.named_scope("sum_rows"):
        near = swap(send, "gc", 1)
        mine = bf16(f32(keep) + f32(near))
        *bits, last = bits_of("gc")[1:]
        for bit in bits:
            order = jnp.arange(len(keep_masks)) ^ (bit >> 1)
            got = swap(mine, "gc", bit).reshape(-1, side, width)[order].reshape(mine.shape)
            mine = bf16(f32(mine) + f32(got))
        got = swap(mine, "gc", last)

    half = width // 2
    with jax.named_scope("dense"):
        activated, message, passed, kept = pl.pallas_call(
            functools.partial(dense_kernel, last >> 1),
            out_shape=[
                block,
                jax.ShapeDtypeStruct(mine.shape, jnp.bfloat16),
                jax.ShapeDtypeStruct((half, width), jnp.bfloat16),
                jax.ShapeDtypeStruct((half, width), jnp.float32),
            ],
            in_specs=[VMEM] * (3 + len(grads)),
            out_specs=[VMEM] * 4,
            scratch_shapes=[pltpu.VMEM((width, width), jnp.float32)],
            compiler_params=params(limit),
        )(mine, got, weight, *[grads[m] for m in keep_masks])

    with jax.named_scope("swap_cores"):
        answer = swap(message, "gc", 1)
        passed = swap(passed, "gc", 1)
        running = kept + f32(after(passed, answer))
    stages = bits_of("gr")[:0:-1] + [1]
    sent, got, order = [], [], Line()

    def launch(running):
        with jax.named_scope("sum_weight"):
            sent.append(bf16(running))
            got.append(swap_crossed(sent[-1], stages[len(sent) - 1]))

    def advance():
        if len(sent) > len(stages):
            return
        with jax.named_scope("sum_weight"):
            running = f32(sent[-1]) + f32(order(got[-1]))
            if len(sent) < len(stages):
                launch(running)
            else:
                sent.append(bf16(running))
                got.append(swap(sent[-1], "gc", 1))

    launch(running)

    with jax.named_scope("backward_blocks"):
        kept_masks = [(m,) for m in far_first[:-1]] + [(2, 0)]
        out_layout = [tuple(m + 1 for m in masks) for masks in kept_masks] + kept_masks
        outs = pl.pallas_call(
            functools.partial(backward_kernel, [keep_masks, send_masks], out_layout),
            out_shape=[stacked(len(masks)) for masks in out_layout],
            in_specs=[SMEM] + [VMEM] * 3,
            out_specs=[VMEM] * len(out_layout),
            scratch_shapes=[
                pltpu.VMEM((gc_size, side, width), jnp.bfloat16),
                pltpu.VMEM((gr_size, side, width), jnp.float32),
            ],
            compiler_params=params(limit),
        )(info, values, message, answer)
        sends, keeps = outs[: len(kept_masks)], outs[len(kept_masks):]

    with jax.named_scope("sum_columns"):
        arrived = [swap(v, "gr", 1) for v in sends]
        order(keeps[0])
        advance()
        parts = []
        for masks, kept, part in zip(kept_masks[:-1], keeps, arrived):
            total = bf16(f32(kept) + f32(order(part)))
            parts += [(m, total[n * side : (n + 1) * side]) for n, m in enumerate(masks)]
        terms = [swap(v, "gr", m) for m, v in parts]
        own = (keeps[-1], order(arrived[-1]))
        total = bf16(f32(own[0][:side]) + f32(own[1][:side]))
        terms.append(swap(total, "gr", 2))
        advance()
    while len(sent) <= len(stages):
        advance()
    terms = [order(term) for term in terms]
    running, other = sent[-1], order(got[-1])

    grad_features, grad_weight = pl.pallas_call(
        finish_kernel,
        out_shape=[
            jax.ShapeDtypeStruct((side, width), jnp.float32),
            jax.ShapeDtypeStruct((width, width), jnp.float32),
        ],
        in_specs=[VMEM] * (4 + len(terms)),
        out_specs=[VMEM] * 2,
        compiler_params=params(limit),
    )(running, other, *own, *terms)
    return activated[None], grad_weight, grad_features[None]


def solution(mesh):
    placed = (
        P("gc", "gr", None),
        P(),
        P("gr", "gc", None),
        P("gr", "gc", None),
        P("gr", "gc", None),
        P("gr", "gc"),
        P("gr", "gc", None, None, None),
    )
    return jax.shard_map(
        per_device,
        mesh=mesh,
        in_specs=placed,
        out_specs=(P("gr", "gc", None), P(), P("gc", "gr", None)),
        check_vma=False,
    )
```
